32 devices in a mesh: seq: 8 (over z, x), mp: 4 (over y, core).
Axes of the slice: x: 2, y: 2, z: 4, core: 2. Of those that a mesh axis runs over, the one named last changes fastest.
Arguments:
- tokens: bfloat16 [4096, 4096], P('seq'), may hold values from -6 to 6
- w_query: bfloat16 [4096, 2048], P(None, 'mp'), may hold values from -0.09375 to 0.09375
- w_key: bfloat16 [4096, 2048], P(None, 'mp'), may hold values from -0.09375 to 0.09375
- w_value: bfloat16 [4096, 2048], P(None, 'mp'), may hold values from -0.09375 to 0.09375
- starts: int32 [6], replicated, may hold values from 1024 to 4095, as said below
- cotangent: bfloat16 [4096, 2048], P('seq', 'mp'), may hold values from -6 to 6
Outputs:
- attended: bfloat16 [4096, 2048], P('seq', 'mp')
- input_grad: bfloat16 [4096, 4096], P(('seq', 'mp'))
- grad_query: float32 [4096, 2048], P('seq', 'mp')
- grad_key: float32 [4096, 2048], P('seq', 'mp')
- grad_value: float32 [4096, 2048], P('seq', 'mp')
The draws below stay inside these ranges and needn't reach their ends.
Inputs may be any that keep to these rules, and one draw needn't show every extreme that they name: The starts rise strictly; start number i (counting from 0) lies at or after 4096 // 4 + i * w and before 4096 // 4 + (i + 1) * w, with w = 512.
All inputs are finite; a program needn't handle non-finite values.
Results may differ from the reference program's by a relative error of at most 0.029.
Values may be sent and summed in bfloat16 or wider, within the bound.
A program may use at most 128 MiB of HBM per device.

```python
import jax
import jax.numpy as jnp
from jax import lax

D = 4096
HEADS = 16
DH = 128
TOK_DEV = 512
NSEG = 6
TOKENS = 4096
HEADS_DEV = 4
N_SEQ = 8
N_MP = 4


def draw_starts(key, part):
    first_pos = TOKENS // 4
    stratum = (TOKENS - first_pos) // NSEG
    offsets = jax.random.randint(key, (NSEG,), 0, stratum)
    return (first_pos + jnp.arange(NSEG, dtype=jnp.int32) * stratum + offsets).astype(jnp.int32)


def spiked(values, stream_key, source, target, blocks, factor):
    def block_of(position):
        return (jnp.arange(values.shape[position]) // (values.shape[position] // blocks)).reshape((-1,) + (1,) * (values.ndim - 1 - position))

    near = jax.random.permutation(stream_key, blocks)[block_of(target)]
    other_side = (block_of(target) + blocks // 2) % blocks
    return jnp.where((block_of(source) == near) | (block_of(source) == other_side), factor * values, values)


def block_scale(own_key, dims, cuts, low, high):
    loudness, own = 1.0, jax.random.fold_in(own_key, 6)
    for position, blocks in cuts:
        draws = jnp.exp(jax.random.uniform(jax.random.fold_in(own, position), (blocks,), jnp.float32, low / len(cuts), high / len(cuts)))
        loudness = loudness * jnp.repeat(draws, dims[position] // blocks).reshape([-1 if axis == position else 1 for axis in range(len(dims))])
    return loudness


def bell_draw(own_key, extent, scale, most, shards=(), kind=jnp.bfloat16):
    array = scale * jax.random.normal(own_key, extent, jnp.float32)
    if shards:
        array = array * block_scale(own_key, extent, shards, -0.22, 0.18)
    return jnp.clip(array, -most, most).astype(kind)


def bell_draw_with(key, dims, scale, reach, shards, heavy, kind=jnp.bfloat16):
    result = scale * jax.random.normal(key, dims, jnp.float32)
    if shards:
        result = result * block_scale(key, dims, shards, -0.22, 0.18)
    return jnp.clip(spiked(result, jax.random.fold_in(key, 3), *heavy), -reach, reach).astype(kind)


def setup_inputs(seed: int = 0) -> dict:
    arg_keys = jax.random.split(jax.random.key(seed), 7)
    tokens = bell_draw_with(arg_keys[0], (TOKENS, D), 1.0, 6.0, ((0, 8),), (0, 1, 8, 2.0))
    w_query = bell_draw(arg_keys[1], (D, HEADS * DH), D ** -0.5, 0.09375, ((1, 4),))
    w_key = bell_draw(arg_keys[2], (D, HEADS * DH), D ** -0.5, 0.09375, ((1, 4),))
    w_value = bell_draw(arg_keys[3], (D, HEADS * DH), D ** -0.5, 0.09375, ((1, 4),))
    starts = draw_starts(jax.random.fold_in(arg_keys[6], 71), 0)
    cotangent = bell_draw(arg_keys[5], (TOKENS, HEADS * DH), 1.0, 6.0, ((0, 8), (1, 4)))
    return {"tokens": tokens, "w_query": w_query, "w_key": w_key, "w_value": w_value, "starts": starts, "cotangent": cotangent}


def span_masks(starts, begin_pos, row_count):
    positions = begin_pos + jnp.arange(row_count, dtype=jnp.int32)
    seg_ids = jnp.sum((starts[None, :] <= positions[:, None]).astype(jnp.int32), axis=1)
    seg_before = jnp.sum((starts < begin_pos).astype(jnp.int32))
    mask_in = (seg_ids == seg_before).astype(jnp.float32)
    mask_out = (seg_ids == seg_ids[-1]).astype(jnp.float32)
    reset_flag = (seg_ids[-1] > seg_before).astype(jnp.float32).reshape(1)
    causal = positions[:, None] >= positions[None, :]
    pair_mask = ((seg_ids[:, None] == seg_ids[None, :]) & causal).astype(jnp.float32)
    return mask_in, mask_out, reset_flag, pair_mask


def summaries(query_heads, key_heads, value_heads, grad_heads, mask_in, mask_out, score_scale):
    keys_kept = key_heads * mask_out.astype(jnp.bfloat16)[None, :, None]
    queries_kept = query_heads * mask_in.astype(jnp.bfloat16)[None, :, None]
    forward_part = score_scale * jnp.einsum("hsd,hse->hde", keys_kept, value_heads, preferred_element_type=jnp.float32)
    backward_part = score_scale * jnp.einsum("htd,hte->hde", queries_kept, grad_heads, preferred_element_type=jnp.float32)
    return forward_part, backward_part


def span_grads(query_heads, key_heads, value_heads, grad_heads, mask_in, mask_out, pair_mask, state_in, reverse_in, score_scale):
    f32 = jnp.float32
    scores = (score_scale * jnp.einsum("htd,hsd->hts", query_heads, key_heads, preferred_element_type=f32) * pair_mask).astype(jnp.bfloat16)
    grad_scores = (score_scale * jnp.einsum("htd,hsd->hts", grad_heads, value_heads, preferred_element_type=f32) * pair_mask).astype(jnp.bfloat16)
    state_low = state_in.astype(jnp.bfloat16)
    state_high = reverse_in.astype(jnp.bfloat16)
    inner = mask_in[None, :, None]
    outer = mask_out[None, :, None]
    attended_heads = jnp.einsum("hts,hsd->htd", scores, value_heads, preferred_element_type=f32) + inner * jnp.einsum("htd,hde->hte", query_heads, state_low, preferred_element_type=f32)
    query_grad = jnp.einsum("hts,hsd->htd", grad_scores, key_heads, preferred_element_type=f32) + inner * jnp.einsum("hte,hde->htd", grad_heads, state_low, preferred_element_type=f32)
    key_grad = jnp.einsum("hts,htd->hsd", grad_scores, query_heads, preferred_element_type=f32) + outer * jnp.einsum("hde,hse->hsd", state_high, value_heads, preferred_element_type=f32)
    value_grad = jnp.einsum("hts,htd->hsd", scores, grad_heads, preferred_element_type=f32) + outer * jnp.einsum("hde,hsd->hse", state_high, key_heads, preferred_element_type=f32)
    return attended_heads, query_grad, key_grad, value_grad


def head_major(matrix):
    row_count = matrix.shape[0]
    return matrix.reshape(row_count, HEADS, DH).transpose(1, 0, 2)


def token_major(tensor):
    return tensor.transpose(1, 0, 2).reshape(tensor.shape[1], -1)


def fold_states(carry_sum, item_pair):
    piece_sum, reset_flag = item_pair
    return piece_sum + (1.0 - reset_flag[0]) * carry_sum, carry_sum


def reference(tokens, w_query, w_key, w_value, starts, cotangent):
    score_scale = 1.0 / DH
    grad_scale = float(TOKENS) ** -0.5
    queries = jnp.dot(tokens, w_query, preferred_element_type=jnp.float32).astype(jnp.bfloat16)
    keys = jnp.dot(tokens, w_key, preferred_element_type=jnp.float32).astype(jnp.bfloat16)
    values = jnp.dot(tokens, w_value, preferred_element_type=jnp.float32).astype(jnp.bfloat16)
    numbers = jnp.arange(N_SEQ, dtype=jnp.int32)

    def rows_of(matrix, span_number):
        return lax.dynamic_slice_in_dim(matrix, (span_number * TOK_DEV).astype(jnp.int32), TOK_DEV, 0)

    def heads_of(span_number):
        return (head_major(rows_of(queries, span_number)), head_major(rows_of(keys, span_number)),
                head_major(rows_of(values, span_number)), head_major(rows_of(cotangent, span_number)))

    def summary_of(span_number):
        mask_in, mask_out, reset_flag, pair_mask = span_masks(starts, span_number * TOK_DEV, TOK_DEV)
        query_heads, key_heads, value_heads, grad_heads = heads_of(span_number)
        forward_part, backward_part = summaries(query_heads, key_heads, value_heads, grad_heads, mask_in, mask_out, score_scale)
        return forward_part, backward_part, reset_flag

    forward_all, backward_all, flags = lax.map(summary_of, numbers)
    zero_state = jnp.zeros((HEADS, DH, DH), jnp.float32)
    _, states_in = lax.scan(fold_states, zero_state, (forward_all, flags))
    _, reverses_in = lax.scan(fold_states, zero_state, (backward_all, flags), reverse=True)
    group_cols = HEADS_DEV * DH
    total_cols = HEADS * DH

    def final_step(weight_sum, item_triple):
        span_number, state_in, reverse_in = item_triple
        mask_in, mask_out, reset_flag, pair_mask = span_masks(starts, span_number * TOK_DEV, TOK_DEV)
        query_heads, key_heads, value_heads, grad_heads = heads_of(span_number)
        attended_heads, query_grad, key_grad, value_grad = span_grads(query_heads, key_heads, value_heads, grad_heads, mask_in, mask_out, pair_mask, state_in, reverse_in, score_scale)
        attended_rows = token_major(attended_heads).astype(jnp.bfloat16)
        query_rows = token_major(query_grad).astype(jnp.bfloat16)
        key_rows = token_major(key_grad).astype(jnp.bfloat16)
        value_rows = token_major(value_grad).astype(jnp.bfloat16)
        grad_block = jnp.concatenate([query_rows, key_rows, value_rows], axis=1)
        token_rows = rows_of(tokens, span_number)
        weight_term = (grad_scale * jnp.dot(token_rows.T, grad_block, preferred_element_type=jnp.float32)).astype(jnp.bfloat16)
        weight_term = lax.optimization_barrier(weight_term).astype(jnp.float32)
        input_sum = jnp.zeros((TOK_DEV, D), jnp.float32)
        for group in range(N_MP):
            low_col = group * group_cols
            high_col = low_col + group_cols
            partial_sum = jnp.dot(query_rows[:, low_col:high_col], w_query[:, low_col:high_col].T, preferred_element_type=jnp.float32)
            partial_sum = partial_sum + jnp.dot(key_rows[:, low_col:high_col], w_key[:, low_col:high_col].T, preferred_element_type=jnp.float32)
            partial_sum = partial_sum + jnp.dot(value_rows[:, low_col:high_col], w_value[:, low_col:high_col].T, preferred_element_type=jnp.float32)
            rounded = lax.optimization_barrier(partial_sum.astype(jnp.bfloat16))
            input_sum = input_sum + rounded.astype(jnp.float32)
        return weight_sum + weight_term, (attended_rows, input_sum.astype(jnp.bfloat16))

    start_sum = jnp.zeros((D, 3 * total_cols), jnp.float32)
    weight_sum, (attended_all, input_all) = lax.scan(final_step, start_sum, (numbers, states_in, reverses_in))
    attended = attended_all.reshape(TOKENS, total_cols)
    input_grad = input_all.reshape(TOKENS, D)
    grad_query = weight_sum[:, :total_cols]
    grad_key = weight_sum[:, total_cols:2 * total_cols]
    grad_value = weight_sum[:, 2 * total_cols:]
    return (attended, input_grad, grad_query, grad_key, grad_value)
```

```python
import jax
import jax.numpy as jnp
from jax import lax
from jax.sharding import PartitionSpec as P

DH = 128


def span_masks(starts, begin_pos, row_count):
    positions = begin_pos + jnp.arange(row_count, dtype=jnp.int32)
    seg_ids = jnp.sum((starts[None, :] <= positions[:, None]).astype(jnp.int32), axis=1)
    seg_before = jnp.sum((starts < begin_pos).astype(jnp.int32))
    mask_in = (seg_ids == seg_before).astype(jnp.float32)
    mask_out = (seg_ids == seg_ids[-1]).astype(jnp.float32)
    reset_flag = (seg_ids[-1] > seg_before).astype(jnp.float32).reshape(1)
    causal = positions[:, None] >= positions[None, :]
    pair_mask = ((seg_ids[:, None] == seg_ids[None, :]) & causal).astype(jnp.float32)
    return (mask_in, mask_out, reset_flag, pair_mask)


def summaries(query_heads, key_heads, value_heads, grad_heads, mask_in, mask_out, score_scale):
    keys_kept = key_heads * mask_out.astype(jnp.bfloat16)[None, :, None]
    queries_kept = query_heads * mask_in.astype(jnp.bfloat16)[None, :, None]
    forward_part = score_scale * jnp.einsum(
        "hsd,hse->hde", keys_kept, value_heads, preferred_element_type=jnp.float32
    )
    backward_part = score_scale * jnp.einsum(
        "htd,hte->hde", queries_kept, grad_heads, preferred_element_type=jnp.float32
    )
    return (forward_part, backward_part)


def span_grads(
    query_heads,
    key_heads,
    value_heads,
    grad_heads,
    mask_in,
    mask_out,
    pair_mask,
    state_in,
    reverse_in,
    score_scale,
):
    f32 = jnp.float32
    scores = (
        score_scale
        * jnp.einsum("htd,hsd->hts", query_heads, key_heads, preferred_element_type=f32)
        * pair_mask
    ).astype(jnp.bfloat16)
    grad_scores = (
        score_scale
        * jnp.einsum("htd,hsd->hts", grad_heads, value_heads, preferred_element_type=f32)
        * pair_mask
    ).astype(jnp.bfloat16)
    state_low = state_in.astype(jnp.bfloat16)
    state_high = reverse_in.astype(jnp.bfloat16)
    inner = mask_in[None, :, None]
    outer = mask_out[None, :, None]
    attended_heads = jnp.einsum(
        "hts,hsd->htd", scores, value_heads, preferred_element_type=f32
    ) + inner * jnp.einsum("htd,hde->hte", query_heads, state_low, preferred_element_type=f32)
    query_grad = jnp.einsum(
        "hts,hsd->htd", grad_scores, key_heads, preferred_element_type=f32
    ) + inner * jnp.einsum("hte,hde->htd", grad_heads, state_low, preferred_element_type=f32)
    key_grad = jnp.einsum(
        "hts,htd->hsd", grad_scores, query_heads, preferred_element_type=f32
    ) + outer * jnp.einsum("hde,hse->hsd", state_high, value_heads, preferred_element_type=f32)
    value_grad = jnp.einsum(
        "hts,htd->hsd", scores, grad_heads, preferred_element_type=f32
    ) + outer * jnp.einsum("hde,hsd->hse", state_high, key_heads, preferred_element_type=f32)
    return (attended_heads, query_grad, key_grad, value_grad)


def head_major(matrix, head_count):
    row_count = matrix.shape[0]
    return matrix.reshape(row_count, head_count, DH).transpose(1, 0, 2)


def token_major(tensor):
    return tensor.transpose(1, 0, 2).reshape(tensor.shape[1], -1)


def linked_pairs(token_count, span_total, start_count):
    first = token_count // 4
    stratum = (token_count - first) // start_count
    size = token_count // span_total

    def possible(low, high):
        begin, end = (low + 1) * size, high * size
        return not any(
            begin <= first + i * stratum and first + (i + 1) * stratum <= end
            for i in range(start_count)
        )

    distances = {}
    for low in range(span_total):
        for high in range(low + 1, span_total):
            if possible(low, high):
                distances.setdefault(high - low, []).append((low, high))
    return distances


def linked_states(forward_part, backward_part, starts, row_count):
    span_total, span_index = lax.axis_size("seq"), lax.axis_index("seq")
    begin = span_index * row_count
    seg_before = jnp.sum((starts < begin).astype(jnp.int32))
    seg_last = jnp.sum((starts < begin + row_count).astype(jnp.int32))
    forward_low = forward_part.astype(jnp.bfloat16)
    backward_low = backward_part.astype(jnp.bfloat16)
    state_in = jnp.zeros_like(forward_part)
    reverse_in = jnp.zeros_like(backward_part)
    pairs_at = linked_pairs(row_count * span_total, span_total, starts.shape[0])
    for distance, pairs in pairs_at.items():
        got = lax.ppermute(forward_low, "seq", pairs)
        source_last = jnp.sum((starts < begin - (distance - 1) * row_count).astype(jnp.int32))
        state_in = state_in + jnp.where(source_last == seg_before, got.astype(jnp.float32), 0.0)
        got = lax.ppermute(backward_low, "seq", [(high, low) for low, high in pairs])
        source_before = jnp.sum((starts < begin + distance * row_count).astype(jnp.int32))
        reverse_in = reverse_in + jnp.where(source_before == seg_last, got.astype(jnp.float32), 0.0)
    return state_in, reverse_in


def line_scatter(parts):
    span_total = lax.axis_size("seq")
    length = span_total // 2
    place = lax.axis_index("seq") // 2

    def part_for(target):
        return lax.dynamic_index_in_dim(parts, jnp.clip(target, 0, length - 1), 0, keepdims=False)

    total = part_for(place).astype(jnp.float32)
    for way in (1, -1):
        carried = None
        for step in range(1, length):
            ahead = way * (length - step)
            sent = part_for(place + ahead)
            if carried is not None:
                sent = (sent.astype(jnp.float32) + carried.astype(jnp.float32)).astype(jnp.bfloat16)
            pairs = [
                (s, s + 2 * way) for s in range(span_total) if 0 <= s // 2 + ahead < length
            ]
            carried = lax.ppermute(sent, "seq", pairs)
        if carried is not None:
            total = total + carried.astype(jnp.float32)
    return total


def halving_scatter(partial):
    count = lax.axis_size("mp")
    index = lax.axis_index("mp")
    size = partial.shape[0] // count

    def pick(k):
        return lax.dynamic_slice_in_dim(partial, jnp.bitwise_xor(index, k) * size, size, 0)

    held = {k: pick(k) for k in range(count)}
    bit = 1
    while bit < count:
        pairs = [(m, m ^ bit) for m in range(count)]
        away = [k for k in held if k & bit]
        sent = jnp.concatenate([held[k] for k in away], axis=0) if len(away) > 1 else held[away[0]]
        got = lax.ppermute(sent, "mp", pairs)
        kind = jnp.bfloat16
        held = {
            k ^ bit: (
                held[k ^ bit].astype(jnp.float32)
                + got[i * size : (i + 1) * size].astype(jnp.float32)
            ).astype(kind)
            for i, k in enumerate(away)
        }
        bit *= 2
    return held[0]


def on_device(tokens, w_query, w_key, w_value, starts, cotangent):
    row_count, width = tokens.shape
    head_count = w_query.shape[1] // DH
    span_total = lax.axis_size("seq")
    span_index = lax.axis_index("seq")
    side = span_index % 2
    length = span_total // 2
    piece = width // span_total
    score_scale = 1.0 / DH
    grad_scale = float(row_count * span_total) ** (-0.5)
    swap = [(s, s ^ 1) for s in range(span_total)]

    def half_columns(which):
        return jnp.concatenate(
            [
                lax.dynamic_slice_in_dim(tokens, (2 * z + which) * piece, piece, 1)
                for z in range(length)
            ],
            axis=1,
        )

    tokens_got = lax.ppermute(half_columns(1 - side), "seq", swap)
    tokens_pair = jnp.concatenate([half_columns(side), tokens_got], axis=0)

    queries = jnp.dot(tokens, w_query, preferred_element_type=jnp.float32).astype(jnp.bfloat16)
    keys = jnp.dot(tokens, w_key, preferred_element_type=jnp.float32).astype(jnp.bfloat16)
    values = jnp.dot(tokens, w_value, preferred_element_type=jnp.float32).astype(jnp.bfloat16)
    mask_in, mask_out, _, pair_mask = span_masks(starts, span_index * row_count, row_count)
    query_heads = head_major(queries, head_count)
    key_heads = head_major(keys, head_count)
    value_heads = head_major(values, head_count)
    grad_heads = head_major(cotangent, head_count)
    forward_part, backward_part = summaries(
        query_heads, key_heads, value_heads, grad_heads, mask_in, mask_out, score_scale
    )
    state_in, reverse_in = linked_states(forward_part, backward_part, starts, row_count)
    attended_heads, query_grad, key_grad, value_grad = span_grads(
        query_heads,
        key_heads,
        value_heads,
        grad_heads,
        mask_in,
        mask_out,
        pair_mask,
        state_in,
        reverse_in,
        score_scale,
    )
    attended = token_major(attended_heads).astype(jnp.bfloat16)
    rows = [token_major(g).astype(jnp.bfloat16) for g in (query_grad, key_grad, value_grad)]
    sums = []
    for own in rows:
        pair = jnp.concatenate([own, lax.ppermute(own, "seq", swap)], axis=0)
        partial = (
            grad_scale
            * jnp.einsum("tc,th->ch", tokens_pair, pair, preferred_element_type=jnp.float32)
        ).astype(jnp.bfloat16)
        sums.append(line_scatter(partial.reshape(length, piece, partial.shape[1])))
    result = jnp.einsum("th,dh->td", rows[0], w_query, preferred_element_type=jnp.float32)
    result = result + jnp.einsum("th,dh->td", rows[1], w_key, preferred_element_type=jnp.float32)
    result = result + jnp.einsum("th,dh->td", rows[2], w_value, preferred_element_type=jnp.float32)
    input_grad = halving_scatter(result.astype(jnp.bfloat16))
    return (attended, input_grad, *sums)


def solution(mesh):
    in_specs = (P("seq", None), P(None, "mp"), P(None, "mp"), P(None, "mp"), P(), P("seq", "mp"))
    out_specs = (
        P("seq", "mp"),
        P(("seq", "mp"), None),
        P("seq", "mp"),
        P("seq", "mp"),
        P("seq", "mp"),
    )
    return jax.shard_map(
        on_device, mesh=mesh, in_specs=in_specs, out_specs=out_specs, check_vma=False
    )
```

```python
import functools

import jax
import jax.numpy as jnp
from jax import lax
from jax.experimental import pallas as pl
from jax.experimental.pallas import tpu as pltpu
from jax.sharding import PartitionSpec as P

DH = 128
F32 = jnp.float32
LOW = jnp.bfloat16


def params():
    return pltpu.CompilerParams(vmem_limit_bytes=48 * 1024 * 1024)


def cost(flops, bytes_accessed):
    return pl.CostEstimate(flops=flops, bytes_accessed=bytes_accessed, transcendentals=0)


def dot(a, b, contract):
    return lax.dot_general(a, b, (contract, ((), ())), preferred_element_type=F32)


def segments(starts_ref, count, begin, shape, dim):
    positions = begin + lax.broadcasted_iota(jnp.int32, shape, dim)
    ids = jnp.zeros(shape, jnp.int32)
    for i in range(count):
        ids = ids + (starts_ref[i] <= positions).astype(jnp.int32)
    return ids


def started(starts_ref, count, before):
    total = jnp.int32(0)
    for i in range(count):
        total = total + (starts_ref[i] < before).astype(jnp.int32)
    return total


def project_kernel(
    count, starts_ref, place_ref, x_ref, wq_ref, wk_ref, wv_ref, c_ref,
    q_ref, k_ref, v_ref, fwd_ref, bwd_ref, acc_ref,
):
    step = pl.program_id(0)
    x = x_ref[...]
    for i, w_ref in enumerate((wq_ref, wk_ref, wv_ref)):
        term = jnp.dot(x, w_ref[...], preferred_element_type=F32)

        @pl.when(step == 0)
        def _():
            acc_ref[i] = term

        @pl.when(step > 0)
        def _():
            acc_ref[i] += term

    @pl.when(step == pl.num_programs(0) - 1)
    def _():
        rows = x_ref.shape[0]
        begin = place_ref[0]
        seg = segments(starts_ref, count, begin, (rows, DH), 0)
        mask_in = seg == started(starts_ref, count, begin)
        mask_out = seg == started(starts_ref, count, begin + rows)
        for h in range(q_ref.shape[1] // DH):
            cols = slice(h * DH, (h + 1) * DH)
            q = acc_ref[0, :, cols].astype(LOW)
            k = acc_ref[1, :, cols].astype(LOW)
            v = acc_ref[2, :, cols].astype(LOW)
            q_ref[:, cols] = q
            k_ref[:, cols] = k
            v_ref[:, cols] = v
            kept = jnp.where(mask_out, k.astype(F32), 0.0).astype(LOW)
            fwd_ref[h] = (dot(kept, v, ((0,), (0,))) * (1.0 / DH)).astype(LOW)
            kept = jnp.where(mask_in, q.astype(F32), 0.0).astype(LOW)
            bwd_ref[h] = (dot(kept, c_ref[:, cols], ((0,), (0,))) * (1.0 / DH)).astype(LOW)


def project(starts, begin, tokens, weights, cotangent):
    rows, width = tokens.shape
    cols = weights[0].shape[1]
    heads = cols // DH
    depth = min(1024, width)
    whole = pl.BlockSpec((rows, cols), lambda i, *_: (0, 0))
    state = pl.BlockSpec((heads, DH, DH), lambda i, *_: (0, 0, 0))
    low = jax.ShapeDtypeStruct((rows, cols), LOW)
    part = jax.ShapeDtypeStruct((heads, DH, DH), LOW)
    return pl.pallas_call(
        functools.partial(project_kernel, starts.shape[0]),
        grid_spec=pltpu.PrefetchScalarGridSpec(
            num_scalar_prefetch=2,
            grid=(width // depth,),
            in_specs=[pl.BlockSpec((rows, depth), lambda i, *_: (0, i))]
            + [pl.BlockSpec((depth, cols), lambda i, *_: (i, 0))] * 3
            + [whole],
            out_specs=[whole] * 3 + [state] * 2,
            scratch_shapes=[pltpu.VMEM((3, rows, cols), F32)],
        ),
        out_shape=[low] * 3 + [part] * 2,
        compiler_params=params(),
        cost_estimate=cost(6 * rows * width * cols, 2 * (rows * width + 3 * width * cols)),
        name="project",
    )(starts, begin, tokens, *weights, cotangent)


def attend_kernel(
    count, starts_ref, place_ref, q_ref, k_ref, v_ref, c_ref, s_ref, r_ref,
    a_ref, dq_ref, dk_ref, dv_ref,
):
    rows = q_ref.shape[0]
    begin = place_ref[0]
    q, k, v, c = q_ref[...], k_ref[...], v_ref[...], c_ref[...]
    state, back = s_ref[0], r_ref[0]
    seg_t = segments(starts_ref, count, begin, (rows, 1), 0)
    seg_s = segments(starts_ref, count, begin, (1, rows), 1)
    at_t = lax.broadcasted_iota(jnp.int32, (rows, rows), 0)
    at_s = lax.broadcasted_iota(jnp.int32, (rows, rows), 1)
    pair = (seg_t == seg_s) & (at_t >= at_s)
    inner = (seg_t == started(starts_ref, count, begin)).astype(F32)
    outer = (seg_t == started(starts_ref, count, begin + rows)).astype(F32)
    scale = 1.0 / DH
    last = ((1,), (1,))
    scores = jnp.where(pair, dot(q, k, last) * scale, 0.0).astype(LOW)
    grads = jnp.where(pair, dot(c, v, last) * scale, 0.0).astype(LOW)
    plain, first = ((1,), (0,)), ((0,), (0,))
    a_ref[...] = (dot(scores, v, plain) + inner * dot(q, state, plain)).astype(LOW)
    dq_ref[...] = (dot(grads, k, plain) + inner * dot(c, state, last)).astype(LOW)
    dk_ref[...] = (dot(grads, q, first) + outer * dot(v, back, last)).astype(LOW)
    dv_ref[...] = (dot(scores, c, first) + outer * dot(k, back, plain)).astype(LOW)


def attend(starts, begin, queries, keys, values, cotangent, state_in, reverse_in):
    rows, cols = queries.shape
    heads = cols // DH
    block = pl.BlockSpec((rows, DH), lambda h, *_: (0, h))
    state = pl.BlockSpec((1, DH, DH), lambda h, *_: (h, 0, 0))
    return pl.pallas_call(
        functools.partial(attend_kernel, starts.shape[0]),
        grid_spec=pltpu.PrefetchScalarGridSpec(
            num_scalar_prefetch=2,
            grid=(heads,),
            in_specs=[block] * 4 + [state] * 2,
            out_specs=[block] * 4,
        ),
        out_shape=[jax.ShapeDtypeStruct((rows, cols), LOW)] * 4,
        compiler_params=params(),
        cost_estimate=cost(heads * 12 * rows * rows * DH, 16 * rows * cols),
        name="attend",
    )(starts, begin, queries, keys, values, cotangent, state_in, reverse_in)


def turn_kernel(list_ref, x_ref, o_ref):
    o_ref[...] = x_ref[...].T


def turn(blocks, tokens, piece):
    rows = tokens.shape[0]
    many = blocks.shape[0]
    return pl.pallas_call(
        turn_kernel,
        grid_spec=pltpu.PrefetchScalarGridSpec(
            num_scalar_prefetch=1,
            grid=(many,),
            in_specs=[pl.BlockSpec((rows, piece), lambda i, at: (0, at[i]))],
            out_specs=pl.BlockSpec((piece, rows), lambda i, at: (i, 0)),
        ),
        out_shape=jax.ShapeDtypeStruct((many * piece, rows), LOW),
        compiler_params=params(),
        cost_estimate=cost(0, 4 * many * piece * rows),
        name="turn",
    )(blocks, tokens)


def share_kernel(half, scale, order_ref, own_ref, near_ref, far_ref, g_ref, h_ref, o_ref):
    step = pl.program_id(0)
    total = jnp.dot(own_ref[...], g_ref[...], preferred_element_type=F32)

    def write(got):
        both = total + jnp.dot(got, h_ref[...], preferred_element_type=F32)
        o_ref[0] = (scale * both).astype(LOW)

    @pl.when(step < half)
    def _():
        write(near_ref[...])

    @pl.when(step >= half)
    def _():
        write(far_ref[...])


def share(order, own, near, far, grad_own, grad_got, scale):
    length = order.shape[0]
    piece = own.shape[0] // length
    rows, cols = grad_own.shape
    half = near.shape[0] // piece
    grad = pl.BlockSpec((rows, cols), lambda i, at: (0, 0))
    return pl.pallas_call(
        functools.partial(share_kernel, half, scale),
        grid_spec=pltpu.PrefetchScalarGridSpec(
            num_scalar_prefetch=1,
            grid=(length,),
            in_specs=[
                pl.BlockSpec((piece, rows), lambda i, at: (at[i], 0)),
                pl.BlockSpec((piece, rows), lambda i, at: (jnp.minimum(i, half - 1), 0)),
                pl.BlockSpec((piece, rows), lambda i, at: (jnp.maximum(i - half, 0), 0)),
                grad,
                grad,
            ],
            out_specs=pl.BlockSpec((1, piece, cols), lambda i, at: (at[i], 0, 0)),
        ),
        out_shape=jax.ShapeDtypeStruct((length, piece, cols), LOW),
        compiler_params=params(),
        cost_estimate=cost(
            4 * length * piece * rows * cols, 2 * (3 * length * piece * rows + 2 * rows * cols)
        ),
        name="share",
    )(order, own, near, far, grad_own, grad_got)


def inputs_kernel(q_ref, k_ref, v_ref, wq_ref, wk_ref, wv_ref, o_ref):
    last = ((1,), (1,))
    total = dot(q_ref[...], wq_ref[...], last)
    total = total + dot(k_ref[...], wk_ref[...], last)
    total = total + dot(v_ref[...], wv_ref[...], last)
    o_ref[...] = total.astype(LOW)


def inputs(grads, weights):
    rows, cols = grads[0].shape
    width = weights[0].shape[0]
    piece = min(512, width)
    return pl.pallas_call(
        inputs_kernel,
        grid=(width // piece,),
        in_specs=[pl.BlockSpec((rows, cols), lambda i: (0, 0))] * 3
        + [pl.BlockSpec((piece, cols), lambda i: (i, 0))] * 3,
        out_specs=pl.BlockSpec((rows, piece), lambda i: (0, i)),
        out_shape=jax.ShapeDtypeStruct((rows, width), LOW),
        compiler_params=params(),
        cost_estimate=cost(6 * rows * width * cols, 2 * (rows * width + 3 * width * cols)),
        name="inputs",
    )(*grads, *weights)


def linked_pairs(token_count, span_total, start_count):
    first = token_count // 4
    stratum = (token_count - first) // start_count
    size = token_count // span_total

    def possible(low, high):
        begin, end = (low + 1) * size, high * size
        return not any(
            begin <= first + i * stratum and first + (i + 1) * stratum <= end
            for i in range(start_count)
        )

    distances = {}
    for low in range(span_total):
        for high in range(low + 1, span_total):
            if possible(low, high):
                distances.setdefault(high - low, []).append((low, high))
    return distances


def linked_states(forward_part, backward_part, starts, row_count):
    span_total, span_index = lax.axis_size("seq"), lax.axis_index("seq")
    begin = span_index * row_count
    seg_before = jnp.sum((starts < begin).astype(jnp.int32))
    seg_last = jnp.sum((starts < begin + row_count).astype(jnp.int32))
    state_in = jnp.zeros(forward_part.shape, jnp.float32)
    reverse_in = jnp.zeros(backward_part.shape, jnp.float32)
    pairs_at = linked_pairs(row_count * span_total, span_total, starts.shape[0])
    for distance, pairs in pairs_at.items():
        got = lax.ppermute(forward_part, "seq", pairs)
        source_last = jnp.sum((starts < begin - (distance - 1) * row_count).astype(jnp.int32))
        state_in = state_in + jnp.where(source_last == seg_before, got.astype(jnp.float32), 0.0)
        got = lax.ppermute(backward_part, "seq", [(high, low) for low, high in pairs])
        source_before = jnp.sum((starts < begin + distance * row_count).astype(jnp.int32))
        reverse_in = reverse_in + jnp.where(source_before == seg_last, got.astype(jnp.float32), 0.0)
    return state_in.astype(jnp.bfloat16), reverse_in.astype(jnp.bfloat16)


def line_scatter(parts):
    span_total = lax.axis_size("seq")
    length = span_total // 2
    place = lax.axis_index("seq") // 2

    def part_for(target):
        return lax.dynamic_index_in_dim(parts, jnp.clip(target, 0, length - 1), 0, keepdims=False)

    total = part_for(place).astype(jnp.float32)
    for way in (1, -1):
        carried = None
        for step in range(1, length):
            ahead = way * (length - step)
            sent = part_for(place + ahead)
            if carried is not None:
                sent = (sent.astype(jnp.float32) + carried.astype(jnp.float32)).astype(jnp.bfloat16)
            pairs = [
                (s, s + 2 * way) for s in range(span_total) if 0 <= s // 2 + ahead < length
            ]
            carried = lax.ppermute(sent, "seq", pairs)
        if carried is not None:
            total = total + carried.astype(jnp.float32)
    return total


def halving_scatter(partial):
    count = lax.axis_size("mp")
    index = lax.axis_index("mp")
    size = partial.shape[0] // count

    def pick(k):
        return lax.dynamic_slice_in_dim(partial, jnp.bitwise_xor(index, k) * size, size, 0)

    held = {k: pick(k) for k in range(count)}
    bit = 1
    while bit < count:
        pairs = [(m, m ^ bit) for m in range(count)]
        away = [k for k in held if k & bit]
        sent = jnp.concatenate([held[k] for k in away], axis=0) if len(away) > 1 else held[away[0]]
        got = lax.ppermute(sent, "mp", pairs)
        kind = jnp.bfloat16
        held = {
            k ^ bit: (
                held[k ^ bit].astype(jnp.float32)
                + got[i * size : (i + 1) * size].astype(jnp.float32)
            ).astype(kind)
            for i, k in enumerate(away)
        }
        bit *= 2
    return held[0]


def on_device(tokens, w_query, w_key, w_value, starts, cotangent):
    row_count, width = tokens.shape
    span_total = lax.axis_size("seq")
    span_index = lax.axis_index("seq")
    side = span_index % 2
    length = span_total // 2
    half = length // 2
    piece = width // span_total
    grad_scale = float(row_count * span_total) ** (-0.5)
    swap = [(s, s ^ 1) for s in range(span_total)]
    mates = [(m, m ^ 1) for m in range(lax.axis_size("mp"))]
    begin = (span_index * row_count).astype(jnp.int32).reshape(1)
    weights = (w_query, w_key, w_value)

    turn_order = jnp.arange(length, dtype=jnp.int32)
    core = (lax.axis_index("mp") % 2).astype(jnp.int32)
    order = (turn_order + half * core) % length
    away = turn(2 * order[:half] + 1 - side, tokens, piece)
    begin, away = lax.optimization_barrier((begin, away))
    near = lax.ppermute(away, "seq", swap)
    far = lax.ppermute(near, "mp", mates)

    queries, keys, values, forward_part, backward_part = project(
        starts, begin, tokens, weights, cotangent
    )
    own = turn(2 * turn_order + side, tokens, piece)
    state_in, reverse_in = linked_states(forward_part, backward_part, starts, row_count)
    attended, *rows = attend(
        starts, begin, queries, keys, values, cotangent, state_in, reverse_in
    )
    got = [lax.ppermute(grad, "seq", swap) for grad in rows]
    shares = [
        share(order, own, near, far, mine, theirs, grad_scale) for mine, theirs in zip(rows, got)
    ]
    rows, shares[0] = lax.optimization_barrier((rows, shares[0]))
    sums = [line_scatter(parts) for parts in shares]
    input_grad = halving_scatter(inputs(rows, weights))
    return (attended, input_grad, *sums)


def solution(mesh):
    in_specs = (P("seq", None), P(None, "mp"), P(None, "mp"), P(None, "mp"), P(), P("seq", "mp"))
    out_specs = (
        P("seq", "mp"),
        P(("seq", "mp"), None),
        P("seq", "mp"),
        P("seq", "mp"),
        P("seq", "mp"),
    )
    return jax.shard_map(
        on_device, mesh=mesh, in_specs=in_specs, out_specs=out_specs, check_vma=False
    )
```

```python
import functools

import jax
import jax.numpy as jnp
from jax import lax
from jax.experimental import pallas as pl
from jax.experimental.pallas import tpu as pltpu
from jax.sharding import PartitionSpec as P

DH = 128
F32 = jnp.float32
LOW = jnp.bfloat16


def params():
    return pltpu.CompilerParams(vmem_limit_bytes=58 * 1024 * 1024)


def cost(flops, bytes_accessed):
    return pl.CostEstimate(flops=flops, bytes_accessed=bytes_accessed, transcendentals=0)


def dot(a, b, contract):
    return lax.dot_general(a, b, (contract, ((), ())), preferred_element_type=F32)


def segments(starts_ref, count, begin, shape, dim):
    positions = begin + lax.broadcasted_iota(jnp.int32, shape, dim)
    ids = jnp.zeros(shape, jnp.int32)
    for i in range(count):
        ids = ids + (starts_ref[i] <= positions).astype(jnp.int32)
    return ids


def started(starts_ref, count, before):
    total = jnp.int32(0)
    for i in range(count):
        total = total + (starts_ref[i] < before).astype(jnp.int32)
    return total


def project_kernel(
    count, starts_ref, place_ref, x_ref, wq_ref, wk_ref, wv_ref, c_ref,
    q_ref, k_ref, v_ref, fwd_ref, bwd_ref, acc_ref,
):
    step = pl.program_id(0)
    x = x_ref[...]
    for i, w_ref in enumerate((wq_ref, wk_ref, wv_ref)):
        term = jnp.dot(x, w_ref[...], preferred_element_type=F32)

        @pl.when(step == 0)
        def _():
            acc_ref[i] = term

        @pl.when(step > 0)
        def _():
            acc_ref[i] += term

    @pl.when(step == pl.num_programs(0) - 1)
    def _():
        rows = x_ref.shape[0]
        begin = place_ref[0]
        seg = segments(starts_ref, count, begin, (rows, DH), 0)
        mask_in = seg == started(starts_ref, count, begin)
        mask_out = seg == started(starts_ref, count, begin + rows)
        for h in range(q_ref.shape[1] // DH):
            cols = slice(h * DH, (h + 1) * DH)
            q = acc_ref[0, :, cols].astype(LOW)
            k = acc_ref[1, :, cols].astype(LOW)
            v = acc_ref[2, :, cols].astype(LOW)
            q_ref[:, cols] = q
            k_ref[:, cols] = k
            v_ref[:, cols] = v
            kept = jnp.where(mask_out, k.astype(F32), 0.0).astype(LOW)
            fwd_ref[h] = (dot(kept, v, ((0,), (0,))) * (1.0 / DH)).astype(LOW)
            kept = jnp.where(mask_in, q.astype(F32), 0.0).astype(LOW)
            bwd_ref[h] = (dot(kept, c_ref[:, cols], ((0,), (0,))) * (1.0 / DH)).astype(LOW)


def project(starts, begin, tokens, weights, cotangent):
    rows, width = tokens.shape
    cols = weights[0].shape[1]
    heads = cols // DH
    depth = min(1024, width)
    whole = pl.BlockSpec((rows, cols), lambda i, *_: (0, 0))
    state = pl.BlockSpec((heads, DH, DH), lambda i, *_: (0, 0, 0))
    low = jax.ShapeDtypeStruct((rows, cols), LOW)
    part = jax.ShapeDtypeStruct((heads, DH, DH), LOW)
    return pl.pallas_call(
        functools.partial(project_kernel, starts.shape[0]),
        grid_spec=pltpu.PrefetchScalarGridSpec(
            num_scalar_prefetch=2,
            grid=(width // depth,),
            in_specs=[pl.BlockSpec((rows, depth), lambda i, *_: (0, i))]
            + [pl.BlockSpec((depth, cols), lambda i, *_: (i, 0))] * 3
            + [whole],
            out_specs=[whole] * 3 + [state] * 2,
            scratch_shapes=[pltpu.VMEM((3, rows, cols), F32)],
        ),
        out_shape=[low] * 3 + [part] * 2,
        compiler_params=params(),
        cost_estimate=cost(6 * rows * width * cols, 2 * (rows * width + 3 * width * cols)),
        name="project",
    )(starts, begin, tokens, *weights, cotangent)


def attend_kernel(
    count, starts_ref, place_ref, q_ref, k_ref, v_ref, c_ref, s_ref, r_ref,
    a_ref, dq_ref, dk_ref, dv_ref,
):
    rows = q_ref.shape[0]
    begin = place_ref[0]
    q, k, v, c = q_ref[...], k_ref[...], v_ref[...], c_ref[...]
    state, back = s_ref[0], r_ref[0]
    seg_t = segments(starts_ref, count, begin, (rows, 1), 0)
    seg_s = segments(starts_ref, count, begin, (1, rows), 1)
    at_t = lax.broadcasted_iota(jnp.int32, (rows, rows), 0)
    at_s = lax.broadcasted_iota(jnp.int32, (rows, rows), 1)
    pair = (seg_t == seg_s) & (at_t >= at_s)
    inner = (seg_t == started(starts_ref, count, begin)).astype(F32)
    outer = (seg_t == started(starts_ref, count, begin + rows)).astype(F32)
    scale = 1.0 / DH
    last = ((1,), (1,))
    scores = jnp.where(pair, dot(q, k, last) * scale, 0.0).astype(LOW)
    grads = jnp.where(pair, dot(c, v, last) * scale, 0.0).astype(LOW)
    plain, first = ((1,), (0,)), ((0,), (0,))
    a_ref[...] = (dot(scores, v, plain) + inner * dot(q, state, plain)).astype(LOW)
    dq_ref[...] = (dot(grads, k, plain) + inner * dot(c, state, last)).astype(LOW)
    dk_ref[...] = (dot(grads, q, first) + outer * dot(v, back, last)).astype(LOW)
    dv_ref[...] = (dot(scores, c, first) + outer * dot(k, back, plain)).astype(LOW)


def attend(starts, begin, queries, keys, values, cotangent, state_in, reverse_in):
    rows, cols = queries.shape
    heads = cols // DH
    block = pl.BlockSpec((rows, DH), lambda h, *_: (0, h))
    state = pl.BlockSpec((1, DH, DH), lambda h, *_: (h, 0, 0))
    return pl.pallas_call(
        functools.partial(attend_kernel, starts.shape[0]),
        grid_spec=pltpu.PrefetchScalarGridSpec(
            num_scalar_prefetch=2,
            grid=(heads,),
            in_specs=[block] * 4 + [state] * 2,
            out_specs=[block] * 4,
        ),
        out_shape=[jax.ShapeDtypeStruct((rows, cols), LOW)] * 4,
        compiler_params=params(),
        cost_estimate=cost(heads * 12 * rows * rows * DH, 16 * rows * cols),
        name="attend",
    )(starts, begin, queries, keys, values, cotangent, state_in, reverse_in)


def turn_kernel(list_ref, x_ref, o_ref):
    o_ref[...] = x_ref[...].T


def turn(blocks, tokens, piece):
    rows = tokens.shape[0]
    many = blocks.shape[0]
    return pl.pallas_call(
        turn_kernel,
        grid_spec=pltpu.PrefetchScalarGridSpec(
            num_scalar_prefetch=1,
            grid=(many,),
            in_specs=[pl.BlockSpec((rows, piece), lambda i, at: (0, at[i]))],
            out_specs=pl.BlockSpec((piece, rows), lambda i, at: (i, 0)),
        ),
        out_shape=jax.ShapeDtypeStruct((many * piece, rows), LOW),
        compiler_params=params(),
        cost_estimate=cost(0, 4 * many * piece * rows),
        name="turn",
    )(blocks, tokens)


def inputs_kernel(q_ref, k_ref, v_ref, wq_ref, wk_ref, wv_ref, o_ref):
    last = ((1,), (1,))
    total = dot(q_ref[...], wq_ref[...], last)
    total = total + dot(k_ref[...], wk_ref[...], last)
    total = total + dot(v_ref[...], wv_ref[...], last)
    o_ref[...] = total.astype(LOW)


def inputs(grads, weights):
    rows, cols = grads[0].shape
    width = weights[0].shape[0]
    piece = min(512, width)
    return pl.pallas_call(
        inputs_kernel,
        grid=(width // piece,),
        in_specs=[pl.BlockSpec((rows, cols), lambda i: (0, 0))] * 3
        + [pl.BlockSpec((piece, cols), lambda i: (i, 0))] * 3,
        out_specs=pl.BlockSpec((rows, piece), lambda i: (0, i)),
        out_shape=jax.ShapeDtypeStruct((rows, width), LOW),
        compiler_params=params(),
        cost_estimate=cost(6 * rows * width * cols, 2 * (rows * width + 3 * width * cols)),
        name="inputs",
    )(*grads, *weights)


def linked_pairs(token_count, span_total, start_count):
    first = token_count // 4
    stratum = (token_count - first) // start_count
    size = token_count // span_total

    def possible(low, high):
        begin, end = (low + 1) * size, high * size
        return not any(
            begin <= first + i * stratum and first + (i + 1) * stratum <= end
            for i in range(start_count)
        )

    distances = {}
    for low in range(span_total):
        for high in range(low + 1, span_total):
            if possible(low, high):
                distances.setdefault(high - low, []).append((low, high))
    return distances


def linked_states(forward_part, backward_part, starts, row_count):
    span_total, span_index = lax.axis_size("seq"), lax.axis_index("seq")
    begin = span_index * row_count
    seg_before = jnp.sum((starts < begin).astype(jnp.int32))
    seg_last = jnp.sum((starts < begin + row_count).astype(jnp.int32))
    state_in = jnp.zeros(forward_part.shape, jnp.float32)
    reverse_in = jnp.zeros(backward_part.shape, jnp.float32)
    pairs_at = linked_pairs(row_count * span_total, span_total, starts.shape[0])
    for distance, pairs in pairs_at.items():
        got = lax.ppermute(forward_part, "seq", pairs)
        source_last = jnp.sum((starts < begin - (distance - 1) * row_count).astype(jnp.int32))
        state_in = state_in + jnp.where(source_last == seg_before, got.astype(jnp.float32), 0.0)
        got = lax.ppermute(backward_part, "seq", [(high, low) for low, high in pairs])
        source_before = jnp.sum((starts < begin + distance * row_count).astype(jnp.int32))
        reverse_in = reverse_in + jnp.where(source_before == seg_last, got.astype(jnp.float32), 0.0)
    return state_in.astype(jnp.bfloat16), reverse_in.astype(jnp.bfloat16)


def flip(index, bit):
    return index + bit - 2 * bit * ((index // bit) % 2)


def finish_kernel(
    length, members, scale, own_ref, near_ref, far_ref, gq_ref, gk_ref, gv_ref, hq_ref, part_ref,
    oq_ref, ok_ref, ov_ref, oi_ref, shares, swapped, carried, bits,
    swap_send, swap_recv, line_send, line_recv, bit_send, bit_recv,
):
    spot, member = lax.axis_index("seq"), lax.axis_index("mp")
    total = 2 * length
    place = spot // 2
    half = length // 2
    shift = half * (member % 2)
    piece = own_ref.shape[0] // length
    size = part_ref.shape[0] // members
    grads = (gq_ref, gk_ref, gv_ref)
    outs = (oq_ref, ok_ref, ov_ref)

    barrier = pltpu.get_barrier_semaphore()
    friends = [
        {"seq": flip(spot, 1)},
        {"seq": (spot + 2) % total},
        {"seq": (spot + total - 2) % total},
    ]
    turns = []
    bit = 1
    while bit < members:
        friends.append({"mp": flip(member, bit)})
        turns.append(bit)
        bit *= 2
    for friend in friends:
        pl.semaphore_signal(barrier, inc=1, device_id=friend, device_id_type=pl.DeviceIdType.MESH)
    pl.semaphore_wait(barrier, len(friends))

    def remote(src, dst, send, recv, where):
        return pltpu.make_async_remote_copy(
            src_ref=src, dst_ref=dst, send_sem=send, recv_sem=recv,
            device_id=where, device_id_type=pl.DeviceIdType.MESH,
        )

    def swap(j):
        return remote(
            grads[j], swapped.at[j - 1], swap_send.at[j - 1], swap_recv.at[j - 1],
            {"seq": flip(spot, 1)},
        )

    def other(k):
        at = member
        for bit in turns:
            if k & bit:
                at = flip(at, bit)
        return pl.ds(pl.multiple_of(at * size, size), size)

    rounds = [[k for k in range(1, members) if k % (2 * b) == b] for b in turns]

    def held(r, k):
        return part_ref.at[other(k)] if r == 0 else bits.at[k + turns[r - 1] - 1]

    def bit_copy(r, k):
        return remote(
            held(r, k), bits.at[k - 1], bit_send.at[k - 1], bit_recv.at[k - 1],
            {"mp": flip(member, turns[r])},
        )

    def bit_start(r):
        for k in rounds[r]:
            bit_copy(r, k).start()

    def bit_end(r):
        for k in rounds[r]:
            bit_copy(r, k).wait()
            both = held(r, k - turns[r])[...].astype(F32) + bits[k - 1].astype(F32)
            bits[k - 1] = both.astype(LOW)

    def share(j):
        mine = grads[j]
        theirs = hq_ref if j == 0 else swapped.at[j - 1]
        for first, got_ref in ((0, near_ref), (half, far_ref)):

            def body(i, _):
                z = (i + first + shift) % length
                rows = pl.ds(pl.multiple_of(z * piece, piece), piece)
                got = got_ref[pl.ds(pl.multiple_of(i * piece, piece), piece), :]
                term = jnp.dot(own_ref[rows, :], mine[...], preferred_element_type=F32)
                term = term + jnp.dot(got, theirs[...], preferred_element_type=F32)
                shares[j, z] = (scale * term).astype(LOW)
                return 0

            lax.fori_loop(0, half, body, 0)

    rank = (place, length - 1 - place)

    def line(step, j, way, first):
        target = place + (length - step if way == 0 else step - length)
        near_by = (spot + (2 if way == 0 else total - 2)) % total
        src = shares.at[j, (target + length) % length] if first else carried.at[way, step - 2, j]
        return remote(
            src, carried.at[way, step - 1, j],
            line_send.at[way, step - 1, j], line_recv.at[way, step - 1, j], {"seq": near_by},
        )

    def send(step, j):
        for way in (0, 1):

            @pl.when(rank[way] == 0)
            def _():
                line(step, j, way, True).start()

            if step > 1:

                @pl.when((rank[way] >= 1) & (rank[way] <= step - 1))
                def _():
                    line(step - 1, j, way, True).wait_recv()
                    target = (place + length + (length - step if way == 0 else step - length)) % length
                    both = carried[way, step - 2, j].astype(F32) + shares[j, target].astype(F32)
                    carried[way, step - 2, j] = both.astype(LOW)
                    line(step, j, way, False).start()

    swap(1).start()
    share(0)
    send(1, 0)
    bit_start(0)
    swap(1).wait()
    swap(2).start()
    share(1)
    send(1, 1)
    bit_end(0)
    bit_start(1)
    swap(2).wait()
    share(2)
    send(1, 2)
    for step in range(2, length):
        for j in range(3):
            send(step, j)
    bit_end(1)
    oi_ref[...] = bits[turns[1] - 1]
    for j in range(3):
        outs[j][...] = shares[j, place].astype(F32)
        for way in (0, 1):

            @pl.when(rank[way] >= 1)
            def _():
                line(length - 1, j, way, True).wait_recv()
                outs[j][...] += carried[way, length - 2, j].astype(F32)

    for step in range(1, length):
        for j in range(3):
            for way in (0, 1):

                @pl.when(rank[way] <= step - 1)
                def _():
                    line(step, j, way, True).wait_send()


def finish(own, near, far, grads, first_got, partial, scale):
    length = lax.axis_size("seq") // 2
    members = lax.axis_size("mp")
    piece = own.shape[0] // length
    rows, cols = grads[0].shape
    size, width = partial.shape[0] // members, partial.shape[1]
    vmem = pl.BlockSpec(memory_space=pltpu.VMEM)
    dma = pltpu.SemaphoreType.DMA
    *sums, input_grad = pl.pallas_call(
        functools.partial(finish_kernel, length, members, scale),
        in_specs=[vmem] * 8,
        out_specs=[vmem] * 4,
        out_shape=[jax.ShapeDtypeStruct((piece, cols), F32)] * 3
        + [jax.ShapeDtypeStruct((size, width), LOW)],
        scratch_shapes=[
            pltpu.VMEM((3, length, piece, cols), LOW),
            pltpu.VMEM((2, rows, cols), LOW),
            pltpu.VMEM((2, length - 1, 3, piece, cols), LOW),
            pltpu.VMEM((members - 1, size, width), LOW),
            dma((2,)), dma((2,)),
            dma((2, length - 1, 3)), dma((2, length - 1, 3)),
            dma((members - 1,)), dma((members - 1,)),
        ],
        compiler_params=pltpu.CompilerParams(
            collective_id=0, has_side_effects=True, vmem_limit_bytes=58 * 1024 * 1024
        ),
        cost_estimate=cost(12 * length * piece * rows * cols, 16 * 1024 * 1024),
        name="finish",
    )(own, near, far, *grads, first_got, partial)
    return sums, input_grad


def on_device(tokens, w_query, w_key, w_value, starts, cotangent):
    row_count, width = tokens.shape
    span_total = lax.axis_size("seq")
    span_index = lax.axis_index("seq")
    side = span_index % 2
    length = span_total // 2
    half = length // 2
    piece = width // span_total
    grad_scale = float(row_count * span_total) ** (-0.5)
    swap = [(s, s ^ 1) for s in range(span_total)]
    mates = [(m, m ^ 1) for m in range(lax.axis_size("mp"))]
    begin = (span_index * row_count).astype(jnp.int32).reshape(1)
    weights = (w_query, w_key, w_value)

    turn_order = jnp.arange(length, dtype=jnp.int32)
    core = (lax.axis_index("mp") % 2).astype(jnp.int32)
    order = (turn_order + half * core) % length
    away = turn(2 * order[:half] + 1 - side, tokens, piece)
    begin, away = lax.optimization_barrier((begin, away))
    near = lax.ppermute(away, "seq", swap)
    far = lax.ppermute(near, "mp", mates)

    queries, keys, values, forward_part, backward_part = project(
        starts, begin, tokens, weights, cotangent
    )
    own = turn(2 * turn_order + side, tokens, piece)
    state_in, reverse_in = linked_states(forward_part, backward_part, starts, row_count)
    begin, own = lax.optimization_barrier((begin, own))
    attended, *rows = attend(
        starts, begin, queries, keys, values, cotangent, state_in, reverse_in
    )
    first_got = lax.ppermute(rows[0], "seq", swap)
    partial = inputs(rows, weights)
    sums, input_grad = finish(own, near, far, rows, first_got, partial, grad_scale)
    return (attended, input_grad, *sums)


def solution(mesh):
    in_specs = (P("seq", None), P(None, "mp"), P(None, "mp"), P(None, "mp"), P(), P("seq", "mp"))
    out_specs = (
        P("seq", "mp"),
        P(("seq", "mp"), None),
        P("seq", "mp"),
        P("seq", "mp"),
        P("seq", "mp"),
    )
    return jax.shard_map(
        on_device, mesh=mesh, in_specs=in_specs, out_specs=out_specs, check_vma=False
    )
```

```python
import functools

import jax
import jax.numpy as jnp
from jax import lax
from jax.experimental import pallas as pl
from jax.experimental.pallas import tpu as pltpu
from jax.sharding import PartitionSpec as P

DH = 128
F32 = jnp.float32
LOW = jnp.bfloat16


def params():
    return pltpu.CompilerParams(vmem_limit_bytes=58 * 1024 * 1024)


def cost(flops, bytes_accessed):
    return pl.CostEstimate(flops=flops, bytes_accessed=bytes_accessed, transcendentals=0)


def dot(a, b, contract):
    return lax.dot_general(a, b, (contract, ((), ())), preferred_element_type=F32)


def segments(starts_ref, count, begin, shape, dim):
    positions = begin + lax.broadcasted_iota(jnp.int32, shape, dim)
    ids = jnp.zeros(shape, jnp.int32)
    for i in range(count):
        ids = ids + (starts_ref[i] <= positions).astype(jnp.int32)
    return ids


def started(starts_ref, count, before):
    total = jnp.int32(0)
    for i in range(count):
        total = total + (starts_ref[i] < before).astype(jnp.int32)
    return total


def project_kernel(
    count, starts_ref, place_ref, x_ref, wq_ref, wk_ref, wv_ref, c_ref,
    q_ref, k_ref, v_ref, fwd_ref, bwd_ref, acc_ref,
):
    step = pl.program_id(0)
    x = x_ref[...]
    for i, w_ref in enumerate((wq_ref, wk_ref, wv_ref)):
        term = jnp.dot(x, w_ref[...], preferred_element_type=F32)

        @pl.when(step == 0)
        def _():
            acc_ref[i] = term

        @pl.when(step > 0)
        def _():
            acc_ref[i] += term

    @pl.when(step == pl.num_programs(0) - 1)
    def _():
        rows = x_ref.shape[0]
        begin = place_ref[0]
        seg = segments(starts_ref, count, begin, (rows, DH), 0)
        mask_in = seg == started(starts_ref, count, begin)
        mask_out = seg == started(starts_ref, count, begin + rows)
        for h in range(q_ref.shape[1] // DH):
            cols = slice(h * DH, (h + 1) * DH)
            q = acc_ref[0, :, cols].astype(LOW)
            k = acc_ref[1, :, cols].astype(LOW)
            v = acc_ref[2, :, cols].astype(LOW)
            q_ref[:, cols] = q
            k_ref[:, cols] = k
            v_ref[:, cols] = v
            kept = jnp.where(mask_out, k.astype(F32), 0.0).astype(LOW)
            fwd_ref[h] = (dot(kept, v, ((0,), (0,))) * (1.0 / DH)).astype(LOW)
            kept = jnp.where(mask_in, q.astype(F32), 0.0).astype(LOW)
            bwd_ref[h] = (dot(kept, c_ref[:, cols], ((0,), (0,))) * (1.0 / DH)).astype(LOW)


def project(starts, begin, tokens, weights, cotangent):
    rows, width = tokens.shape
    cols = weights[0].shape[1]
    heads = cols // DH
    depth = min(1024, width)
    whole = pl.BlockSpec((rows, cols), lambda i, *_: (0, 0))
    state = pl.BlockSpec((heads, DH, DH), lambda i, *_: (0, 0, 0))
    low = jax.ShapeDtypeStruct((rows, cols), LOW)
    part = jax.ShapeDtypeStruct((heads, DH, DH), LOW)
    return pl.pallas_call(
        functools.partial(project_kernel, starts.shape[0]),
        grid_spec=pltpu.PrefetchScalarGridSpec(
            num_scalar_prefetch=2,
            grid=(width // depth,),
            in_specs=[pl.BlockSpec((rows, depth), lambda i, *_: (0, i))]
            + [pl.BlockSpec((depth, cols), lambda i, *_: (i, 0))] * 3
            + [whole],
            out_specs=[whole] * 3 + [state] * 2,
            scratch_shapes=[pltpu.VMEM((3, rows, cols), F32)],
        ),
        out_shape=[low] * 3 + [part] * 2,
        compiler_params=params(),
        cost_estimate=cost(6 * rows * width * cols, 2 * (rows * width + 3 * width * cols)),
        name="project",
    )(starts, begin, tokens, *weights, cotangent)


def attend_kernel(
    count, starts_ref, place_ref, q_ref, k_ref, v_ref, c_ref, s_ref, r_ref,
    a_ref, dq_ref, dk_ref, dv_ref,
):
    rows = q_ref.shape[0]
    begin = place_ref[0]
    q, k, v, c = q_ref[...], k_ref[...], v_ref[...], c_ref[...]
    state, back = s_ref[0], r_ref[0]
    seg_t = segments(starts_ref, count, begin, (rows, 1), 0)
    seg_s = segments(starts_ref, count, begin, (1, rows), 1)
    at_t = lax.broadcasted_iota(jnp.int32, (rows, rows), 0)
    at_s = lax.broadcasted_iota(jnp.int32, (rows, rows), 1)
    pair = (seg_t == seg_s) & (at_t >= at_s)
    inner = (seg_t == started(starts_ref, count, begin)).astype(F32)
    outer = (seg_t == started(starts_ref, count, begin + rows)).astype(F32)
    scale = 1.0 / DH
    last = ((1,), (1,))
    scores = jnp.where(pair, dot(q, k, last) * scale, 0.0).astype(LOW)
    grads = jnp.where(pair, dot(c, v, last) * scale, 0.0).astype(LOW)
    plain, first = ((1,), (0,)), ((0,), (0,))
    a_ref[...] = (dot(scores, v, plain) + inner * dot(q, state, plain)).astype(LOW)
    dq_ref[...] = (dot(grads, k, plain) + inner * dot(c, state, last)).astype(LOW)
    dk_ref[...] = (dot(grads, q, first) + outer * dot(v, back, last)).astype(LOW)
    dv_ref[...] = (dot(scores, c, first) + outer * dot(k, back, plain)).astype(LOW)


def attend(starts, begin, queries, keys, values, cotangent, state_in, reverse_in):
    rows, cols = queries.shape
    heads = cols // DH
    block = pl.BlockSpec((rows, DH), lambda h, *_: (0, h))
    state = pl.BlockSpec((1, DH, DH), lambda h, *_: (h, 0, 0))
    return pl.pallas_call(
        functools.partial(attend_kernel, starts.shape[0]),
        grid_spec=pltpu.PrefetchScalarGridSpec(
            num_scalar_prefetch=2,
            grid=(heads,),
            in_specs=[block] * 4 + [state] * 2,
            out_specs=[block] * 4,
        ),
        out_shape=[jax.ShapeDtypeStruct((rows, cols), LOW)] * 4,
        compiler_params=params(),
        cost_estimate=cost(heads * 12 * rows * rows * DH, 16 * rows * cols),
        name="attend",
    )(starts, begin, queries, keys, values, cotangent, state_in, reverse_in)


def turn_kernel(list_ref, x_ref, o_ref):
    o_ref[...] = x_ref[...].T


def turn(blocks, tokens, piece):
    rows = tokens.shape[0]
    many = blocks.shape[0]
    return pl.pallas_call(
        turn_kernel,
        grid_spec=pltpu.PrefetchScalarGridSpec(
            num_scalar_prefetch=1,
            grid=(many,),
            in_specs=[pl.BlockSpec((rows, piece), lambda i, at: (0, at[i]))],
            out_specs=pl.BlockSpec((piece, rows), lambda i, at: (i, 0)),
        ),
        out_shape=jax.ShapeDtypeStruct((many * piece, rows), LOW),
        compiler_params=params(),
        cost_estimate=cost(0, 4 * many * piece * rows),
        name="turn",
    )(blocks, tokens)


def linked_pairs(token_count, span_total, start_count):
    first = token_count // 4
    stratum = (token_count - first) // start_count
    size = token_count // span_total

    def possible(low, high):
        begin, end = (low + 1) * size, high * size
        return not any(
            begin <= first + i * stratum and first + (i + 1) * stratum <= end
            for i in range(start_count)
        )

    distances = {}
    for low in range(span_total):
        for high in range(low + 1, span_total):
            if possible(low, high):
                distances.setdefault(high - low, []).append((low, high))
    return distances


def linked_states(forward_part, backward_part, starts, row_count):
    span_total, span_index = lax.axis_size("seq"), lax.axis_index("seq")
    begin = span_index * row_count
    seg_before = jnp.sum((starts < begin).astype(jnp.int32))
    seg_last = jnp.sum((starts < begin + row_count).astype(jnp.int32))
    state_in = jnp.zeros(forward_part.shape, jnp.float32)
    reverse_in = jnp.zeros(backward_part.shape, jnp.float32)
    pairs_at = linked_pairs(row_count * span_total, span_total, starts.shape[0])
    for distance, pairs in pairs_at.items():
        got = lax.ppermute(forward_part, "seq", pairs)
        source_last = jnp.sum((starts < begin - (distance - 1) * row_count).astype(jnp.int32))
        state_in = state_in + jnp.where(source_last == seg_before, got.astype(jnp.float32), 0.0)
        got = lax.ppermute(backward_part, "seq", [(high, low) for low, high in pairs])
        source_before = jnp.sum((starts < begin + distance * row_count).astype(jnp.int32))
        reverse_in = reverse_in + jnp.where(source_before == seg_last, got.astype(jnp.float32), 0.0)
    return state_in.astype(jnp.bfloat16), reverse_in.astype(jnp.bfloat16)


def flip(index, bit):
    return index + bit - 2 * bit * ((index // bit) % 2)


def finish_kernel(
    length, members, scale, own_hbm, near_hbm, far_hbm, gq_ref, gk_ref, gv_ref, wq_hbm, wk_hbm,
    wv_hbm, oq_ref, ok_ref, ov_ref, oi_ref, own_ref, near_ref, far_ref, wide, part_ref, shares,
    swapped, carried, bits, load_sem, swap_send, swap_recv, line_send, line_recv, bit_send, bit_recv,
):
    spot, member = lax.axis_index("seq"), lax.axis_index("mp")
    total = 2 * length
    place = spot // 2
    half = length // 2
    shift = half * (member % 2)
    piece = own_ref.shape[0] // length
    size = part_ref.shape[0] // members
    grads = (gq_ref, gk_ref, gv_ref)
    outs = (oq_ref, ok_ref, ov_ref)

    loads = [
        pltpu.make_async_copy(src, dst, load_sem.at[i])
        for i, (src, dst) in enumerate(
            [
                (wq_hbm, wide.at[0]),
                (wk_hbm, wide.at[1]),
                (wv_hbm, wide.at[2]),
                (own_hbm, own_ref),
                (near_hbm, near_ref),
                (far_hbm, far_ref),
            ]
        )
    ]
    for load in loads:
        load.start()

    barrier = pltpu.get_barrier_semaphore()
    friends = [
        {"seq": flip(spot, 1)},
        {"seq": (spot + 2) % total},
        {"seq": (spot + total - 2) % total},
    ]
    turns = []
    bit = 1
    while bit < members:
        friends.append({"mp": flip(member, bit)})
        turns.append(bit)
        bit *= 2
    for friend in friends:
        pl.semaphore_signal(barrier, inc=1, device_id=friend, device_id_type=pl.DeviceIdType.MESH)
    pl.semaphore_wait(barrier, len(friends))

    def remote(src, dst, send, recv, where):
        return pltpu.make_async_remote_copy(
            src_ref=src, dst_ref=dst, send_sem=send, recv_sem=recv,
            device_id=where, device_id_type=pl.DeviceIdType.MESH,
        )

    def swap(j):
        return remote(
            grads[j], swapped.at[j], swap_send.at[j], swap_recv.at[j],
            {"seq": flip(spot, 1)},
        )

    def other(k):
        at = member
        for bit in turns:
            if k & bit:
                at = flip(at, bit)
        return pl.ds(pl.multiple_of(at * size, size), size)

    rounds = [[k for k in range(1, members) if k % (2 * b) == b] for b in turns]

    def held(r, k):
        return part_ref.at[other(k)] if r == 0 else bits.at[k + turns[r - 1] - 1]

    def bit_copy(r, k):
        return remote(
            held(r, k), bits.at[k - 1], bit_send.at[k - 1], bit_recv.at[k - 1],
            {"mp": flip(member, turns[r])},
        )

    def bit_start(r):
        for k in rounds[r]:
            bit_copy(r, k).start()

    def bit_end(r):
        for k in rounds[r]:
            bit_copy(r, k).wait()
            both = held(r, k - turns[r])[...].astype(F32) + bits[k - 1].astype(F32)
            bits[k - 1] = both.astype(LOW)

    def share(j):
        mine = grads[j]
        theirs = swapped.at[j]
        for first, got_ref in ((0, near_ref), (half, far_ref)):

            def body(i, _):
                z = (i + first + shift) % length
                rows = pl.ds(pl.multiple_of(z * piece, piece), piece)
                got = got_ref[pl.ds(pl.multiple_of(i * piece, piece), piece), :]
                term = jnp.dot(own_ref[rows, :], mine[...], preferred_element_type=F32)
                term = term + jnp.dot(got, theirs[...], preferred_element_type=F32)
                shares[j, z] = (scale * term).astype(LOW)
                return 0

            lax.fori_loop(0, half, body, 0)

    rank = (place, length - 1 - place)

    def line(step, j, way, first):
        target = place + (length - step if way == 0 else step - length)
        near_by = (spot + (2 if way == 0 else total - 2)) % total
        src = shares.at[j, (target + length) % length] if first else carried.at[way, step - 2, j]
        return remote(
            src, carried.at[way, step - 1, j],
            line_send.at[way, step - 1, j], line_recv.at[way, step - 1, j], {"seq": near_by},
        )

    def send(step, j):
        for way in (0, 1):

            @pl.when(rank[way] == 0)
            def _():
                line(step, j, way, True).start()

            if step > 1:

                @pl.when((rank[way] >= 1) & (rank[way] <= step - 1))
                def _():
                    line(step - 1, j, way, True).wait_recv()
                    target = (place + length + (length - step if way == 0 else step - length)) % length
                    both = carried[way, step - 2, j].astype(F32) + shares[j, target].astype(F32)
                    carried[way, step - 2, j] = both.astype(LOW)
                    line(step, j, way, False).start()

    swap(0).start()
    for load in loads[:3]:
        load.wait()
    width = wide.shape[1]
    strip = min(512, width)

    def strips(i, _):
        at = pl.ds(pl.multiple_of(i * strip, strip), strip)
        term = dot(gq_ref[...], wide[0, at, :], ((1,), (1,)))
        term = term + dot(gk_ref[...], wide[1, at, :], ((1,), (1,)))
        term = term + dot(gv_ref[...], wide[2, at, :], ((1,), (1,)))
        part_ref[:, at] = term.astype(LOW)
        return 0

    lax.fori_loop(0, width // strip, strips, 0)
    for load in loads[3:]:
        load.wait()
    swap(0).wait()
    swap(1).start()
    share(0)
    send(1, 0)
    bit_start(0)
    swap(1).wait()
    swap(2).start()
    share(1)
    send(1, 1)
    bit_end(0)
    bit_start(1)
    swap(2).wait()
    share(2)
    send(1, 2)
    for step in range(2, length):
        for j in range(3):
            send(step, j)
    bit_end(1)
    oi_ref[...] = bits[turns[1] - 1]
    for j in range(3):
        outs[j][...] = shares[j, place].astype(F32)
        for way in (0, 1):

            @pl.when(rank[way] >= 1)
            def _():
                line(length - 1, j, way, True).wait_recv()
                outs[j][...] += carried[way, length - 2, j].astype(F32)

    for step in range(1, length):
        for j in range(3):
            for way in (0, 1):

                @pl.when(rank[way] <= step - 1)
                def _():
                    line(step, j, way, True).wait_send()


def finish(own, near, far, grads, weights, scale):
    length = lax.axis_size("seq") // 2
    members = lax.axis_size("mp")
    piece = own.shape[0] // length
    rows, cols = grads[0].shape
    size, width = rows // members, weights[0].shape[0]
    vmem = pl.BlockSpec(memory_space=pltpu.VMEM)
    hbm = pl.BlockSpec(memory_space=pl.ANY)
    dma = pltpu.SemaphoreType.DMA
    *sums, input_grad = pl.pallas_call(
        functools.partial(finish_kernel, length, members, scale),
        in_specs=[hbm] * 3 + [vmem] * 3 + [hbm] * 3,
        out_specs=[vmem] * 4,
        out_shape=[jax.ShapeDtypeStruct((piece, cols), F32)] * 3
        + [jax.ShapeDtypeStruct((size, width), LOW)],
        scratch_shapes=[
            pltpu.VMEM(own.shape, LOW),
            pltpu.VMEM(near.shape, LOW),
            pltpu.VMEM(far.shape, LOW),
            pltpu.VMEM((3, width, cols), LOW),
            pltpu.VMEM((rows, width), LOW),
            pltpu.VMEM((3, length, piece, cols), LOW),
            pltpu.VMEM((3, rows, cols), LOW),
            pltpu.VMEM((2, length - 1, 3, piece, cols), LOW),
            pltpu.VMEM((members - 1, size, width), LOW),
            dma((6,)),
            dma((3,)), dma((3,)),
            dma((2, length - 1, 3)), dma((2, length - 1, 3)),
            dma((members - 1,)), dma((members - 1,)),
        ],
        compiler_params=pltpu.CompilerParams(
            collective_id=0, has_side_effects=True, vmem_limit_bytes=58 * 1024 * 1024
        ),
        cost_estimate=cost(12 * length * piece * rows * cols, 16 * 1024 * 1024),
        name="finish",
    )(own, near, far, *grads, *weights)
    return sums, input_grad


def on_device(tokens, w_query, w_key, w_value, starts, cotangent):
    row_count, width = tokens.shape
    span_total = lax.axis_size("seq")
    span_index = lax.axis_index("seq")
    side = span_index % 2
    length = span_total // 2
    half = length // 2
    piece = width // span_total
    grad_scale = float(row_count * span_total) ** (-0.5)
    swap = [(s, s ^ 1) for s in range(span_total)]
    mates = [(m, m ^ 1) for m in range(lax.axis_size("mp"))]
    begin = (span_index * row_count).astype(jnp.int32).reshape(1)
    weights = (w_query, w_key, w_value)

    turn_order = jnp.arange(length, dtype=jnp.int32)
    core = (lax.axis_index("mp") % 2).astype(jnp.int32)
    order = (turn_order + half * core) % length
    away = turn(2 * order[:half] + 1 - side, tokens, piece)
    begin, away = lax.optimization_barrier((begin, away))
    near = lax.ppermute(away, "seq", swap)
    far = lax.ppermute(near, "mp", mates)

    queries, keys, values, forward_part, backward_part = project(
        starts, begin, tokens, weights, cotangent
    )
    own = turn(2 * turn_order + side, tokens, piece)
    state_in, reverse_in = linked_states(forward_part, backward_part, starts, row_count)
    begin, own = lax.optimization_barrier((begin, own))
    attended, *rows = attend(
        starts, begin, queries, keys, values, cotangent, state_in, reverse_in
    )
    sums, input_grad = finish(own, near, far, rows, weights, grad_scale)
    return (attended, input_grad, *sums)


def solution(mesh):
    in_specs = (P("seq", None), P(None, "mp"), P(None, "mp"), P(None, "mp"), P(), P("seq", "mp"))
    out_specs = (
        P("seq", "mp"),
        P(("seq", "mp"), None),
        P("seq", "mp"),
        P("seq", "mp"),
        P("seq", "mp"),
    )
    return jax.shard_map(
        on_device, mesh=mesh, in_specs=in_specs, out_specs=out_specs, check_vma=False
    )
```
